256 devices in a mesh: row: 16 (over x, y), col: 16 (over z, core).
Axes of the slice: x: 4, y: 4, z: 8, core: 2. Of those that a mesh axis runs over, the one named last changes fastest.
Arguments:
- entities: bfloat16 [65536, 512], P(('row', 'col')), may hold values from -6 to 6
- entity_bias: bfloat16 [8, 65536], P(None, ('row', 'col')), may hold values from -2 to 250
- w_query: bfloat16 [512, 512], replicated, may hold values from -0.5 to 0.5
- w_key: bfloat16 [512, 512], replicated, may hold values from -0.5 to 0.5
- w_value: bfloat16 [512, 512], replicated, may hold values from -0.25 to 0.25
- w_out: bfloat16 [512, 512], replicated, may hold values from -0.25 to 0.25
- tile_index: int32 [512, 16, 6], P('row', 'col'), may hold values from 0 to 31, as said below
- tile_count: int32 [512, 16], P('row', 'col'), may hold values from 1 to 6, as said below
Outputs:
- updated: float32 [65536, 512], P(('row', 'col'))
The draws below stay inside these ranges and needn't reach their ends.
Inputs may be any that keep to these rules, and one draw needn't show every extreme that they name: `tile_index`: each list holds 6 distinct tile numbers of its source group; slots at or after the count are ignored. `tile_count`: every destination block of 32 tiles has, in each source group, one list with 6 live slots and one with a single live slot.
All inputs are finite; a program needn't handle non-finite values.
Results may differ from the reference program's by a relative error of at most 0.013.
Values may be sent and summed in bfloat16 or wider, within the bound.
No kernel may reach another device: no remote copies, remote signals or barrier semaphores. Data moves between devices by JAX's collectives and lax.ppermute only.
A program may use at most 128 MiB of HBM per device.

```python
import math
import jax
import jax.numpy as jnp
from jax import lax

D = 512
H = 8
HD = 64
TILE = 128
MAXT = 6
ENT_DEV = 256
ENTITIES = 65536
GROUPS = 16
GROUP_ENT = 4096
SRC_TILES = 32
DST_TILES = 512
DT_DEV = 32


def draw_entity_bias(key, part):
    first = jax.random.fold_in(key, 0)
    base = jax.random.uniform(first, (H, ENTITIES), jnp.float32, -2.0, 2.0)
    return base.astype(jnp.bfloat16)


def draw_tile_index(key, part):
    key_list = jax.random.split(key, DST_TILES * GROUPS)
    picked = jax.vmap(lambda single: jax.random.permutation(single, SRC_TILES)[:MAXT])(key_list)
    return picked.reshape(DST_TILES, GROUPS, MAXT).astype(jnp.int32)


def draw_tile_count(key, part):
    first, second, third = jax.random.split(jax.random.fold_in(key, 7), 3)
    blocks = DST_TILES // DT_DEV
    counts = jax.random.randint(first, (blocks, DT_DEV, GROUPS), 1, MAXT + 1)
    full_pos = jax.random.randint(second, (blocks, GROUPS), 0, DT_DEV)
    single_pos = (full_pos + 1 + jax.random.randint(third, (blocks, GROUPS), 0, DT_DEV - 1)) % DT_DEV
    position = jnp.arange(DT_DEV, dtype=jnp.int32)[None, :, None]
    counts = jnp.where(position == full_pos[:, None, :], MAXT, counts)
    counts = jnp.where(position == single_pos[:, None, :], 1, counts)
    return counts.reshape(DST_TILES, GROUPS).astype(jnp.int32)


def steps_of(key, extent, pieces, least, high):
    factor_of, own = 1.0, jax.random.fold_in(key, 6)
    for dim, parts in pieces:
        steps = jnp.exp(jax.random.uniform(jax.random.fold_in(own, dim), (parts,), jnp.float32, least / len(pieces), high / len(pieces)))
        factor_of = factor_of * jnp.repeat(steps, extent[dim] // parts).reshape([-1 if axis == dim else 1 for axis in range(len(extent))])
    return factor_of


def normal_values(key, shape, spread, limit, shards=(), kind=jnp.bfloat16):
    entries = spread * jax.random.normal(key, shape, jnp.float32)
    if shards:
        entries = entries * steps_of(key, shape, shards, -0.22, 0.18)
    return jnp.clip(entries, -limit, limit).astype(kind)


def setup_inputs(seed: int = 0) -> dict:
    keys = jax.random.split(jax.random.key(seed), 9)
    return {
        "entities": normal_values(keys[0], (ENTITIES, D), 1.0, 6.0, ((0, 256),)),
        "entity_bias": draw_entity_bias(jax.random.fold_in(keys[8], 71), 0),
        "w_query": normal_values(keys[2], (D, D), (D // 4) ** -0.5, 0.5),
        "w_key": normal_values(keys[3], (D, D), (D // 4) ** -0.5, 0.5),
        "w_value": normal_values(keys[4], (D, D), D ** -0.5, 0.25),
        "w_out": normal_values(keys[5], (D, D), D ** -0.5, 0.25),
        "tile_index": draw_tile_index(jax.random.fold_in(keys[8], 71), 0),
        "tile_count": draw_tile_count(jax.random.fold_in(keys[8], 71), 0),
    }


def rms_norm(activations):
    values_f = activations.astype(jnp.float32)
    scale_inv = lax.rsqrt(lax.optimization_barrier(jnp.mean(values_f * values_f, axis=-1, keepdims=True)) + 1e-06)
    return (values_f * scale_inv).astype(jnp.bfloat16)

def reference(entities, entity_bias, w_query, w_key, w_value, w_out, tile_index, tile_count):
    normed = rms_norm(entities)
    query_rows = jnp.dot(normed, w_query, preferred_element_type=jnp.float32).astype(jnp.bfloat16)
    key_all = jnp.dot(normed, w_key, preferred_element_type=jnp.float32).astype(jnp.bfloat16)
    value_all = jnp.dot(normed, w_value, preferred_element_type=jnp.float32).astype(jnp.bfloat16)
    member = jnp.arange(GROUP_ENT, dtype=jnp.int32)
    column = jnp.arange(GROUPS, dtype=jnp.int32)
    source_ids = (member[None, :] // ENT_DEV * GROUPS + column[:, None]) * ENT_DEV + member[None, :] % ENT_DEV
    group_keys = key_all[source_ids].reshape(GROUPS, SRC_TILES, TILE, H, HD)
    group_values = value_all[source_ids].reshape(GROUPS, SRC_TILES, TILE, H, HD)
    group_bias = entity_bias[:, source_ids].reshape(H, GROUPS, SRC_TILES, TILE)
    query_tiles = query_rows.reshape(DST_TILES, TILE, H, HD)
    score_scale = 1.0 / math.sqrt(HD)
    slot_pos = jnp.arange(MAXT, dtype=jnp.int32)

    def one_tile(inputs):
        query_tile, tile_ids, counts = inputs
        near_keys = group_keys[column[:, None], tile_ids].reshape(GROUPS, MAXT * TILE, H, HD)
        near_values = group_values[column[:, None], tile_ids].reshape(GROUPS, MAXT * TILE, H, HD)
        near_bias = group_bias[:, column[:, None], tile_ids].reshape(H, GROUPS, MAXT * TILE)
        scores = jnp.einsum('qhd,ckhd->chqk', query_tile.astype(jnp.float32), near_keys.astype(jnp.float32)) * score_scale
        scores = scores + jnp.transpose(near_bias, (1, 0, 2))[:, :, None, :].astype(jnp.float32)
        live_slots = jnp.repeat(slot_pos[None, :] < counts[:, None], TILE, axis=1)[:, None, None, :]
        group_peak = lax.optimization_barrier(jnp.max(jnp.where(live_slots, scores, -1e+30), axis=-1))
        weight = jnp.where(live_slots, jnp.exp(scores - group_peak[..., None]), 0.0)
        group_total = lax.optimization_barrier(jnp.sum(weight, axis=-1))
        weight_b = weight.astype(jnp.bfloat16)
        group_num = jnp.einsum('chqk,ckhd->chqd', weight_b.astype(jnp.float32), near_values.astype(jnp.float32))
        row_peak = lax.optimization_barrier(jnp.max(group_peak, axis=0))
        factor = jnp.exp(group_peak - row_peak[None])
        numerator = lax.optimization_barrier(jnp.sum(factor[..., None] * group_num, axis=0))
        denominator = lax.optimization_barrier(jnp.sum(factor * group_total, axis=0))
        attended = (numerator / denominator[..., None]).astype(jnp.bfloat16)
        return jnp.transpose(attended, (1, 0, 2)).reshape(TILE, D)
    attended = lax.map(one_tile, (query_tiles, tile_index, tile_count)).reshape(DST_TILES * TILE, D)
    return entities.astype(jnp.float32) + jnp.dot(attended, w_out, preferred_element_type=jnp.float32)
```

```python
import functools
import math

import jax
import jax.numpy as jnp
from jax import lax
from jax.experimental import pallas as pl
from jax.experimental.pallas import tpu as pltpu
from jax.sharding import PartitionSpec as P

TILE = 128
MAXT = 6
H = 8
HD = 64
D = 512
OWN = 256
PAY = OWN + 16
ROWS = 16
RING = 8
BLOCKS = ROWS * 2
SLOTS = BLOCKS * 2
VROWS = 80
ACC = D + 48
LOG2E = math.log2(math.e)
F32 = jnp.float32
BF16 = jnp.bfloat16
NEG = -1e30


def split3(x):
    hi = x.astype(BF16)
    rest = x - hi.astype(F32)
    mid = rest.astype(BF16)
    low = (rest - mid.astype(F32)).astype(BF16)
    return hi, mid, low


def source_kernel(src, wk_ref, wvt_ref, k_ref, v_ref, buf, sem):
    def fetch(b, slot):
        return pltpu.make_async_copy(src.at[b], buf.at[slot], sem.at[slot])

    row = lax.broadcasted_iota(jnp.int32, (16, TILE), 0)
    ones_rows = jnp.where(row == 0, 1.0, 0.0).astype(BF16)
    r = lax.broadcasted_iota(jnp.int32, (32, 512), 0)
    c = lax.broadcasted_iota(jnp.int32, (32, 512), 1)
    piece, head = r // 8, r % 8
    target = (head // 2) * 128 + 3 * (head % 2) + piece
    select = jnp.where((c == target) & (piece < 3), 1.0, 0.0).astype(BF16)

    col = lax.broadcasted_iota(jnp.int32, (TILE, 256), 1)
    empty = jnp.where((col == 128) | (col == 131), NEG, 0.0).astype(BF16)
    for p in range(4):
        k_ref[SLOTS, :, p * 256 : (p + 1) * 256] = empty
    v_ref[SLOTS] = jnp.zeros((H * VROWS, TILE), BF16)

    fetch(0, 0).start()

    def step(b, carry):
        slot = lax.rem(b, 2)

        @pl.when(b + 1 < BLOCKS)
        def _():
            fetch(b + 1, 1 - slot).start()

        fetch(b, slot).wait()
        x = buf[slot, 0:OWN, :].astype(F32)
        scale = lax.rsqrt(jnp.mean(x * x, axis=-1, keepdims=True) + 1e-06)
        normed = (x * scale).astype(BF16)
        keys = jnp.dot(normed, wk_ref[...], preferred_element_type=F32).astype(BF16)
        vals = lax.dot_general(
            wvt_ref[...], normed, (((1,), (1,)), ((), ())), preferred_element_type=F32
        ).astype(BF16)
        prior = buf[slot, OWN : OWN + 16, 0:OWN].astype(F32)[0:8] * LOG2E
        hi, mid, low = split3(prior)
        stack = jnp.concatenate(
            [hi.astype(F32), mid.astype(F32), low.astype(F32), jnp.zeros((8, OWN), F32)], axis=0
        ).astype(BF16)
        aux = lax.dot_general(
            stack, select, (((0,), (0,)), ((), ())), preferred_element_type=F32
        ).astype(BF16)
        for half in range(2):
            rows = slice(half * TILE, (half + 1) * TILE)
            for p in range(4):
                k_ref[2 * b + half, :, p * 256 : p * 256 + 128] = keys[rows, p * 128 : (p + 1) * 128]
                k_ref[2 * b + half, :, p * 256 + 128 : (p + 1) * 256] = aux[rows, p * 128 : (p + 1) * 128]
            for h in range(H):
                v_ref[2 * b + half, h * VROWS : h * VROWS + HD, :] = vals[h * HD : (h + 1) * HD, rows]
                v_ref[2 * b + half, h * VROWS + HD : (h + 1) * VROWS, :] = ones_rows
        return carry

    lax.fori_loop(0, BLOCKS, step, 0)


def project_source(src, w_key, w_value_t):
    return pl.pallas_call(
        source_kernel,
        out_shape=(
            pltpu.VMEM((SLOTS + 1, TILE, 1024), BF16),
            pltpu.VMEM((SLOTS + 1, H * VROWS, TILE), BF16),
        ),
        in_specs=[
            pl.BlockSpec(memory_space=pl.ANY),
            pl.BlockSpec(memory_space=pltpu.VMEM),
            pl.BlockSpec(memory_space=pltpu.VMEM),
        ],
        out_specs=(pl.BlockSpec(memory_space=pltpu.VMEM), pl.BlockSpec(memory_space=pltpu.VMEM)),
        scratch_shapes=[pltpu.VMEM((2, PAY, D), BF16), pltpu.SemaphoreType.DMA((2,))],
        compiler_params=pltpu.CompilerParams(vmem_limit_bytes=12 * 1024 * 1024),
        cost_estimate=pl.CostEstimate(
            flops=2 * BLOCKS * OWN * D * D * 2, bytes_accessed=BLOCKS * PAY * D * 2, transcendentals=0
        ),
        name="project_source",
    )(src, w_key, w_value_t)


def chunk_kernel(chunk, list_ref, pair_ref, q_ref, k_ref, v_ref, prev_ref, out_ref, rhs, s_scr, acc):
    del prev_ref
    row = lax.broadcasted_iota(jnp.int32, (TILE, 256), 0)
    col = lax.broadcasted_iota(jnp.int32, (TILE, 256), 1)
    ones = jnp.where((row < 3) & (col < 128) | (row >= 3) & (row < 6) & (col >= 128), 1.0, 0.0)
    for p in range(4):
        rhs[p, 0:HD, 128:256] = jnp.zeros((HD, 128), BF16)
        rhs[p, HD:128, 0:128] = jnp.zeros((HD, 128), BF16)
        rhs[p, 128:256, :] = ones.astype(BF16)
    for half in range(2):
        lanes = slice(half * TILE, (half + 1) * TILE)
        for p in range(4):
            rhs[p, 0:HD, 0:128] = q_ref[p * 128 : p * 128 + HD, lanes]
            rhs[p, HD:128, 128:256] = q_ref[p * 128 + HD : (p + 1) * 128, lanes]
        acc[...] = jnp.zeros(acc.shape, F32)
        pairs = pair_ref[chunk * 2 + half]
        base = (chunk * 2 + half) * 2 * MAXT

        def score(it, peaks):
            tiles = (list_ref[base + 2 * it], list_ref[base + 2 * it + 1])
            found = []
            for p in range(4):
                best = peaks[p]
                for j in range(2):
                    s = jnp.dot(
                        k_ref[tiles[j], :, p * 256 : (p + 1) * 256], rhs[p], preferred_element_type=F32
                    )
                    s_scr[it, p, j * TILE : (j + 1) * TILE, :] = s
                    best = jnp.maximum(best, jnp.max(s.reshape(16, 8, 256), axis=0))
                found.append(best)
            return tuple(found)

        peaks = lax.fori_loop(0, pairs, score, tuple(jnp.full((8, 256), -3e38, F32) for _ in range(4)))
        peaks = [jnp.max(x, axis=0, keepdims=True) for x in peaks]

        def weigh(it, carry):
            tiles = (list_ref[base + 2 * it], list_ref[base + 2 * it + 1])
            for p in range(4):
                w = jnp.exp2(s_scr[it, p] - peaks[p]).astype(BF16)
                for g in range(2):
                    h = 2 * p + g
                    rows = slice(h * VROWS, (h + 1) * VROWS)
                    v = jnp.concatenate([v_ref[tiles[0], rows, :], v_ref[tiles[1], rows, :]], axis=1)
                    acc[rows, :] += jnp.dot(v, w[:, g * 128 : (g + 1) * 128], preferred_element_type=F32)
            return carry

        lax.fori_loop(0, pairs, weigh, 0)
        for h in range(H):
            out_ref[h * HD : (h + 1) * HD, lanes] = acc[h * VROWS : h * VROWS + HD, :].astype(BF16)
        total = jnp.concatenate([acc[h * VROWS + HD : h * VROWS + HD + 1, :] for h in range(H)], axis=0)
        peak = jnp.concatenate([peaks[h // 2][:, (h % 2) * 128 : (h % 2 + 1) * 128] for h in range(H)], axis=0)
        t_hi, t_mid, _ = split3(total)
        p_hi, p_mid, p_low = split3(peak)
        pieces = [x.astype(F32) for x in (t_hi, t_mid, p_hi, p_mid, p_low)] + [jnp.zeros((8, TILE), F32)]
        out_ref[D:ACC, lanes] = jnp.concatenate(pieces, axis=0).astype(BF16)


def attend_chunk(chunk, lists, pairs, queries, keys, values, prev):
    return pl.pallas_call(
        functools.partial(chunk_kernel, chunk),
        out_shape=jax.ShapeDtypeStruct((ACC, OWN), BF16),
        in_specs=[
            pl.BlockSpec(memory_space=pltpu.SMEM),
            pl.BlockSpec(memory_space=pltpu.SMEM),
            pl.BlockSpec(memory_space=pltpu.VMEM),
            pl.BlockSpec(memory_space=pltpu.VMEM),
            pl.BlockSpec(memory_space=pltpu.VMEM),
            pl.BlockSpec(memory_space=pl.ANY),
        ],
        out_specs=pl.BlockSpec(memory_space=pltpu.VMEM),
        scratch_shapes=[
            pltpu.VMEM((4, 256, 256), BF16),
            pltpu.VMEM((MAXT, 4, 256, 256), F32),
            pltpu.VMEM((H * VROWS, TILE), F32),
        ],
        compiler_params=pltpu.CompilerParams(vmem_limit_bytes=16 * 1024 * 1024),
        cost_estimate=pl.CostEstimate(flops=4_000_000_000, bytes_accessed=1_000_000, transcendentals=0),
        name="attend_chunk",
    )(lists, pairs, queries, keys, values, prev)


def merge_kernel(*refs):
    parts, (ent_ref, w_ref, out_ref, att) = refs[:RING], refs[RING:]

    def rows(ref, i):
        return ref[D + 8 * i : D + 8 * i + 8, :].astype(F32)

    peaks, totals = [], []
    for ref in parts:
        aux = ref[D:ACC, :].astype(F32)
        totals.append(aux[0:8] + aux[8:16])
        peaks.append(aux[16:24] + aux[24:32] + aux[32:40])
    top = functools.reduce(jnp.maximum, peaks)
    factors = [jnp.exp2(x - top) for x in peaks]
    total = functools.reduce(jnp.add, [f * t for f, t in zip(factors, totals)])
    factors = [f / total for f in factors]
    for h in range(H):
        num = functools.reduce(
            jnp.add,
            [
                ref[h * HD : (h + 1) * HD, :].astype(F32) * f[h : h + 1, :]
                for ref, f in zip(parts, factors)
            ],
        )
        att[h * HD : (h + 1) * HD, :] = num.astype(BF16)
    out_ref[...] = ent_ref[...].astype(F32) + lax.dot_general(
        att[...], w_ref[...], (((0,), (0,)), ((), ())), preferred_element_type=F32
    )


def merge(parts, entities, w_out):
    return pl.pallas_call(
        merge_kernel,
        out_shape=jax.ShapeDtypeStruct((OWN, D), F32),
        in_specs=[pl.BlockSpec(memory_space=pltpu.VMEM)] * (RING + 2),
        out_specs=pl.BlockSpec(memory_space=pltpu.VMEM),
        scratch_shapes=[pltpu.VMEM((D, OWN), BF16)],
        compiler_params=pltpu.CompilerParams(vmem_limit_bytes=16 * 1024 * 1024),
        cost_estimate=pl.CostEstimate(flops=2 * OWN * D * D, bytes_accessed=3_000_000, transcendentals=0),
        name="merge",
    )(*parts, entities, w_out)


def along_z(k):
    return [(z * 2 + c, ((z + k) % RING) * 2 + c) for z in range(RING) for c in range(2)]


def across_cores():
    return [(z * 2 + c, z * 2 + 1 - c) for z in range(RING) for c in range(2)]


def neighbour_lists(tile_index, tile_count):
    me = lax.axis_index("col")
    core, z = me % 2, me // 2
    packed = jnp.concatenate([tile_index[:, 0, :], tile_count], axis=1).reshape(RING, 2, 2, MAXT + 1)
    own = lax.dynamic_index_in_dim(packed, core, 1, keepdims=False)
    other = lax.dynamic_index_in_dim(packed, 1 - core, 1, keepdims=False)
    came = lax.ppermute(other, "col", across_cores())
    first = jnp.where(core == 0, own, came)
    second = jnp.where(core == 0, came, own)

    def slots(x, group):
        t = x[..., :MAXT]
        return (t // 2 * 2 + group) * 2 + t % 2

    n0, n1 = first[..., MAXT:], second[..., MAXT:]
    pos = lax.broadcasted_iota(jnp.int32, (1, 1, 2 * MAXT), 2)
    both = jnp.concatenate([slots(first, 0), slots(second, 1)], axis=-1)
    pick = jnp.where(pos < n0, pos, MAXT + pos - n0)
    source = lax.broadcasted_iota(jnp.int32, (1, 1, 1, 2 * MAXT), 3)
    chosen = jnp.sum(jnp.where(pick[..., None] == source, both[..., None, :], 0), axis=-1)
    chosen = jnp.where(pos < n0 + n1, chosen, SLOTS)
    pairs = (n0 + n1 + 1)[..., 0] // 2
    chosen = jnp.roll(chosen, -z, axis=0)
    pairs = jnp.roll(pairs, -z, axis=0)
    return chosen.reshape(-1), pairs.reshape(-1)


def body(entities, entity_bias, w_query, w_key, w_value, w_out, tile_index, tile_count):
    payload = jnp.concatenate([entities, jnp.pad(entity_bias, ((0, 8), (0, D - OWN)))], axis=0)
    groups = [[r * 16 + z * 2 + c for r in range(ROWS) for c in range(2)] for z in range(RING)]
    source = lax.all_gather(payload, ("row", "col"), axis=0, tiled=False, axis_index_groups=groups)

    x = entities.astype(F32)
    normed = (x * lax.rsqrt(jnp.mean(x * x, axis=-1, keepdims=True) + 1e-06)).astype(BF16)
    queries = (
        lax.dot_general(w_query, normed, (((0,), (1,)), ((), ())), preferred_element_type=F32)
        * (LOG2E / math.sqrt(HD))
    ).astype(BF16)
    order = (4, 3, -3, 2, -2, 1, -1, 0)
    held = {k: lax.ppermute(queries, "col", along_z(-k)) if k else queries for k in order}
    lists, pairs = neighbour_lists(tile_index, tile_count)

    keys, values = project_source(source, w_key, w_value.T)
    prev = lists
    parts = []
    for k in order:
        prev = attend_chunk(k % RING, lists, pairs, held[k], keys, values, prev)
        parts.append(lax.ppermute(prev, "col", along_z(k)) if k else prev)
    return merge(parts, entities, w_out)


def solution(mesh):
    placed = (
        P(("row", "col"), None),
        P(None, ("row", "col")),
        P(),
        P(),
        P(),
        P(),
        P("row", "col", None),
        P("row", "col"),
    )
    return jax.shard_map(
        body, mesh=mesh, in_specs=placed, out_specs=P(("row", "col"), None), check_vma=False
    )
```

```python
import functools
import math

import jax
import jax.numpy as jnp
from jax import lax
from jax.experimental import pallas as pl
from jax.experimental.pallas import tpu as pltpu
from jax.sharding import PartitionSpec as P

TILE = 128
MAXT = 6
H = 8
HD = 64
D = 512
OWN = 256
PAY = OWN + 16
ROWS = 16
RING = 8
BLOCKS = ROWS * 2
SLOTS = BLOCKS * 2
VROWS = 80
VBASE = D + TILE
KVROWS = VBASE + H * VROWS
ACC = D + 48
LOG2E = math.log2(math.e)
F32 = jnp.float32
BF16 = jnp.bfloat16
NEG = -1e30
GANG = 4


def split3(x):
    hi = x.astype(BF16)
    rest = x - hi.astype(F32)
    mid = rest.astype(BF16)
    low = (rest - mid.astype(F32)).astype(BF16)
    return hi, mid, low


def source_kernel(src, wk_hbm, wvt_ref, *rest):
    kv_ref, buf, wk_ref, sem, wk_sem = rest[-5:]

    def fetch(b):
        return pltpu.make_async_copy(src.at[b], buf.at[b], sem.at[b])

    weights = pltpu.make_async_copy(wk_hbm, wk_ref, wk_sem)
    weights.start()
    for b in range(BLOCKS):
        fetch(b).start()
    row = lax.broadcasted_iota(jnp.int32, (16, TILE), 0)
    ones_rows = jnp.where(row == 0, 1.0, 0.0).astype(BF16)
    r = lax.broadcasted_iota(jnp.int32, (32, 128), 0)
    c = lax.broadcasted_iota(jnp.int32, (32, 128), 1)
    select = jnp.where((c == r) & (r < 24), 1.0, 0.0).astype(BF16)

    col = lax.broadcasted_iota(jnp.int32, (TILE, TILE), 1)
    kv_ref[SLOTS] = jnp.zeros((KVROWS, TILE), BF16)
    kv_ref[SLOTS, D : D + TILE, :] = jnp.where(col < 8, NEG, 0.0).astype(BF16)
    weights.wait()

    def step(i, carry):
        for j in range(GANG):
            fetch(GANG * i + j).wait()
        normed = jnp.concatenate([buf[GANG * i + j, 0:OWN, :] for j in range(GANG)], axis=0)
        keys = jnp.dot(normed, wk_ref[...], preferred_element_type=F32).astype(BF16)
        vals = lax.dot_general(
            wvt_ref[...], normed, (((1,), (1,)), ((), ())), preferred_element_type=F32
        ).astype(BF16)
        prior = jnp.concatenate(
            [buf[GANG * i + j, OWN : OWN + 16, 0:OWN].astype(F32)[0:8] for j in range(GANG)], axis=1
        )
        hi, mid, low = split3(prior * LOG2E)
        stack = jnp.concatenate(
            [hi.astype(F32), mid.astype(F32), low.astype(F32), jnp.zeros((8, GANG * OWN), F32)], axis=0
        ).astype(BF16)
        aux = lax.dot_general(
            stack, select, (((0,), (0,)), ((), ())), preferred_element_type=F32
        ).astype(BF16)
        for j in range(2 * GANG):
            rows = slice(j * TILE, (j + 1) * TILE)
            t = 2 * GANG * i + j
            for p in range(4):
                kv_ref[t, p * TILE : (p + 1) * TILE, :] = keys[rows, p * 128 : (p + 1) * 128]
            kv_ref[t, D : D + TILE, :] = aux[rows, :]
            for h in range(H):
                at = VBASE + h * VROWS
                kv_ref[t, at : at + HD, :] = vals[h * HD : (h + 1) * HD, rows]
                kv_ref[t, at + HD : at + VROWS, :] = ones_rows
        return carry

    lax.fori_loop(0, BLOCKS // GANG, step, 0)


def project_source(src, w_key, w_value_t, ready):
    return pl.pallas_call(
        source_kernel,
        out_shape=pltpu.VMEM((SLOTS + 1, KVROWS, TILE), BF16),
        in_specs=[
            pl.BlockSpec(memory_space=pl.ANY),
            pl.BlockSpec(memory_space=pl.ANY),
            pl.BlockSpec(memory_space=pltpu.VMEM),
        ]
        + [pl.BlockSpec(memory_space=pl.ANY)] * len(ready),
        out_specs=pl.BlockSpec(memory_space=pltpu.VMEM),
        scratch_shapes=[
            pltpu.VMEM((BLOCKS, PAY, D), BF16),
            pltpu.VMEM((D, D), BF16),
            pltpu.SemaphoreType.DMA((BLOCKS,)),
            pltpu.SemaphoreType.DMA,
        ],
        compiler_params=pltpu.CompilerParams(vmem_limit_bytes=32 * 1024 * 1024),
        cost_estimate=pl.CostEstimate(
            flops=2 * BLOCKS * OWN * D * D * 2, bytes_accessed=BLOCKS * PAY * D * 2, transcendentals=0
        ),
        name="project_source",
    )(src, w_key, w_value_t, *ready)


def chunk_kernel(chunk, list_ref, pair_ref, q_ref, kv_ref, prev_ref, out_ref, rhs, acc, top, s_scr):
    del prev_ref
    row = lax.broadcasted_iota(jnp.int32, (TILE, 256), 0)
    col = lax.broadcasted_iota(jnp.int32, (TILE, 256), 1)
    for p in range(4):
        head = 2 * p + col // 128
        rhs[p, 0:HD, 128:256] = jnp.zeros((HD, 128), BF16)
        rhs[p, HD:128, 0:128] = jnp.zeros((HD, 128), BF16)
        rhs[p, 128:256, :] = jnp.where((row < 24) & (row % 8 == head), 1.0, 0.0).astype(BF16)

    def tile(half, carry):
        lanes = pl.ds(pl.multiple_of(half * TILE, TILE), TILE)
        for p in range(4):
            rhs[p, 0:HD, 0:128] = q_ref[p * 128 : p * 128 + HD, lanes]
            rhs[p, HD:128, 128:256] = q_ref[p * 128 + HD : (p + 1) * 128, lanes]
        base = (chunk * 2 + half) * 2 * MAXT

        def walk(count):
            tiles = [list_ref[base + j] for j in range(count)]
            peaks = [None] * 4

            def score(p):
                keys = jnp.concatenate(
                    [
                        jnp.concatenate([kv_ref[t, p * TILE : (p + 1) * TILE, :], kv_ref[t, D : D + TILE, :]], axis=1)
                        for t in tiles
                    ],
                    axis=0,
                )
                s = jnp.dot(keys, rhs[p], preferred_element_type=F32)
                s_scr[p, 0 : count * TILE, :] = s
                best = jnp.max(s.reshape(count * TILE // 8, 8, 256), axis=0)
                peaks[p] = jnp.max(best, axis=0, keepdims=True)
                top[p : p + 1, :] = peaks[p]

            def weigh(p):
                w = jnp.exp2(s_scr[p, 0 : count * TILE, :] - peaks[p]).astype(BF16)
                for g in range(2):
                    h = 2 * p + g
                    at = slice(VBASE + h * VROWS, VBASE + (h + 1) * VROWS)
                    v = jnp.concatenate([kv_ref[t, at, :] for t in tiles], axis=1)
                    o = jnp.dot(v, w[:, g * 128 : (g + 1) * 128], preferred_element_type=F32)
                    out_ref[h * HD : (h + 1) * HD, lanes] = o[0:HD, :].astype(BF16)
                    acc[h : h + 1, :] = o[HD : HD + 1, :]

            for p in range(4):
                score(p)
            for p in range(4):
                weigh(p)

        steps = (pair_ref[chunk * 2 + half] + 1) // 2
        for v in range(3):

            @pl.when(steps == v + 1)
            def _():
                walk(4 * (v + 1))

        peak = jnp.concatenate(
            [top[h // 2 : h // 2 + 1, (h % 2) * 128 : (h % 2 + 1) * 128] for h in range(H)], axis=0
        )
        t_hi, t_mid, _ = split3(acc[...])
        p_hi, p_mid, p_low = split3(peak)
        pieces = [x.astype(F32) for x in (t_hi, t_mid, p_hi, p_mid, p_low)] + [jnp.zeros((8, TILE), F32)]
        out_ref[D:ACC, lanes] = jnp.concatenate(pieces, axis=0).astype(BF16)
        return carry

    lax.fori_loop(0, 2, tile, 0)


def attend_chunk(chunk, lists, pairs, queries, source, prev):
    return pl.pallas_call(
        functools.partial(chunk_kernel, chunk),
        out_shape=jax.ShapeDtypeStruct((ACC, OWN), BF16),
        in_specs=[
            pl.BlockSpec(memory_space=pltpu.SMEM),
            pl.BlockSpec(memory_space=pltpu.SMEM),
            pl.BlockSpec(memory_space=pltpu.VMEM),
            pl.BlockSpec(memory_space=pltpu.VMEM),
            pl.BlockSpec(memory_space=pl.ANY),
        ],
        out_specs=pl.BlockSpec(memory_space=pltpu.VMEM),
        scratch_shapes=[
            pltpu.VMEM((4, 256, 256), BF16),
            pltpu.VMEM((H, TILE), F32),
            pltpu.VMEM((8, 256), F32),
            pltpu.VMEM((4, 2 * MAXT * TILE, 256), F32),
        ],
        compiler_params=pltpu.CompilerParams(vmem_limit_bytes=14 * 1024 * 1024),
        cost_estimate=pl.CostEstimate(flops=100_000_000, bytes_accessed=100_000, transcendentals=0),
        name="attend_chunk",
    )(lists, pairs, queries, source, prev)


def combine(parts):
    peaks, totals = [], []
    for ref in parts:
        aux = ref[D:ACC, :].astype(F32)
        totals.append(aux[0:8] + aux[8:16])
        peaks.append(aux[16:24] + aux[24:32] + aux[32:40])
    peak = functools.reduce(jnp.maximum, peaks)
    factors = [jnp.exp2(x - peak) for x in peaks]
    total = functools.reduce(jnp.add, [f * t for f, t in zip(factors, totals)])
    return factors, total, peak


def weighted(parts, factors, h):
    terms = [r[h * HD : (h + 1) * HD, :].astype(F32) * f[h : h + 1, :] for r, f in zip(parts, factors)]
    return functools.reduce(jnp.add, terms)


def join_kernel(a_ref, b_ref, prev_ref, out_ref):
    del prev_ref
    parts = (a_ref, b_ref)
    factors, total, peak = combine(parts)
    for h in range(H):
        out_ref[h * HD : (h + 1) * HD, :] = weighted(parts, factors, h).astype(BF16)
    t_hi, t_mid, _ = split3(total)
    p_hi, p_mid, p_low = split3(peak)
    pieces = [x.astype(F32) for x in (t_hi, t_mid, p_hi, p_mid, p_low)] + [jnp.zeros((8, OWN), F32)]
    out_ref[D:ACC, :] = jnp.concatenate(pieces, axis=0).astype(BF16)


def join(came, own, prev):
    return pl.pallas_call(
        join_kernel,
        out_shape=jax.ShapeDtypeStruct((ACC, OWN), BF16),
        in_specs=[pl.BlockSpec(memory_space=pltpu.VMEM)] * 2 + [pl.BlockSpec(memory_space=pl.ANY)],
        out_specs=pl.BlockSpec(memory_space=pltpu.VMEM),
        compiler_params=pltpu.CompilerParams(vmem_limit_bytes=14 * 1024 * 1024),
        cost_estimate=pl.CostEstimate(flops=1_000_000, bytes_accessed=100_000, transcendentals=0),
        name="join",
    )(came, own, prev)


def merge_kernel(*refs):
    parts, (ent_ref, w_ref, out_ref, att) = refs[:-4], refs[-4:]
    factors, total, _ = combine(parts)
    factors = [f / total for f in factors]
    for h in range(H):
        att[h * HD : (h + 1) * HD, :] = weighted(parts, factors, h).astype(BF16)
    out_ref[...] = ent_ref[...].astype(F32) + lax.dot_general(
        att[...], w_ref[...], (((0,), (0,)), ((), ())), preferred_element_type=F32
    )


def merge(parts, entities, w_out):
    return pl.pallas_call(
        merge_kernel,
        out_shape=jax.ShapeDtypeStruct((OWN, D), F32),
        in_specs=[pl.BlockSpec(memory_space=pltpu.VMEM)] * (len(parts) + 2),
        out_specs=pl.BlockSpec(memory_space=pltpu.VMEM),
        scratch_shapes=[pltpu.VMEM((D, OWN), BF16)],
        compiler_params=pltpu.CompilerParams(vmem_limit_bytes=14 * 1024 * 1024),
        cost_estimate=pl.CostEstimate(flops=2 * OWN * D * D, bytes_accessed=3_000_000, transcendentals=0),
        name="merge",
    )(*parts, entities, w_out)


def along_z(k):
    return [(z * 2 + c, ((z + k) % RING) * 2 + c) for z in range(RING) for c in range(2)]


def across_cores():
    return [(z * 2 + c, z * 2 + 1 - c) for z in range(RING) for c in range(2)]


def neighbour_lists(tile_index, tile_count):
    me = lax.axis_index("col")
    core, z = me % 2, me // 2
    packed = jnp.concatenate([tile_index[:, 0, :], tile_count], axis=1).reshape(RING, 2, 2, MAXT + 1)
    own = lax.dynamic_index_in_dim(packed, core, 1, keepdims=False)
    other = lax.dynamic_index_in_dim(packed, 1 - core, 1, keepdims=False)
    came = lax.ppermute(other, "col", across_cores())
    first = jnp.where(core == 0, own, came)
    second = jnp.where(core == 0, came, own)

    def slots(x, group):
        t = x[..., :MAXT]
        return (t // 2 * 2 + group) * 2 + t % 2

    n0, n1 = first[..., MAXT:], second[..., MAXT:]
    pos = lax.broadcasted_iota(jnp.int32, (1, 1, 2 * MAXT), 2)
    both = jnp.concatenate([slots(first, 0), slots(second, 1)], axis=-1)
    pick = jnp.where(pos < n0, pos, MAXT + pos - n0)
    source = lax.broadcasted_iota(jnp.int32, (1, 1, 1, 2 * MAXT), 3)
    chosen = jnp.sum(jnp.where(pick[..., None] == source, both[..., None, :], 0), axis=-1)
    chosen = jnp.where(pos < n0 + n1, chosen, SLOTS)
    pairs = (n0 + n1 + 1)[..., 0] // 2
    chosen = jnp.roll(chosen, -z, axis=0)
    pairs = jnp.roll(pairs, -z, axis=0)
    return chosen.reshape(-1), pairs.reshape(-1)


def body(entities, entity_bias, w_query, w_key, w_value, w_out, tile_index, tile_count):
    x = entities.astype(F32)
    normed = (x * lax.rsqrt(jnp.mean(x * x, axis=-1, keepdims=True) + 1e-06)).astype(BF16)
    payload = jnp.concatenate([normed, jnp.pad(entity_bias, ((0, 8), (0, D - OWN)))], axis=0)
    groups = [[r * 16 + z * 2 + c for r in range(ROWS) for c in range(2)] for z in range(RING)]
    source = lax.all_gather(payload, ("row", "col"), axis=0, tiled=False, axis_index_groups=groups)

    queries = (
        lax.dot_general(w_query, normed, (((0,), (1,)), ((), ())), preferred_element_type=F32)
        * (LOG2E / math.sqrt(HD))
    ).astype(BF16)
    order = (4, 3, -3, 2, -2, 1, -1, 0)
    held = {k: lax.ppermute(queries, "col", along_z(-k)) if k else queries for k in order}
    lists, pairs = neighbour_lists(tile_index, tile_count)

    held_all = [held[k] for k in order if k]
    source = project_source(source, w_key, w_value.T, held_all)
    last = [lists]

    def chunk(k):
        last[0] = attend_chunk(k % RING, lists, pairs, held[k], source, last[0])
        return last[0]

    def joined(came, own):
        last[0] = join(came, own, last[0])
        return last[0]

    down, up = -1, 1
    send = lambda x, way: lax.ppermute(x, "col", along_z(way))
    low = send(chunk(4), down)
    high = send(chunk(3), up)
    for step in (3, 2):
        own_low, own_high = chunk(-step), chunk(step - 1)
        low = send(joined(low, own_low), down)
        high = send(joined(high, own_high), up)
    own_low, own = chunk(-1), chunk(0)
    low = send(joined(low, own_low), down)
    return merge((own, high, low), entities, w_out)


def solution(mesh):
    placed = (
        P(("row", "col"), None),
        P(None, ("row", "col")),
        P(),
        P(),
        P(),
        P(),
        P("row", "col", None),
        P("row", "col"),
    )
    return jax.shard_map(
        body, mesh=mesh, in_specs=placed, out_specs=P(("row", "col"), None), check_vma=False
    )
```

```python
import functools
import math

import jax
import jax.numpy as jnp
from jax import lax
from jax.experimental import pallas as pl
from jax.experimental.pallas import tpu as pltpu
from jax.sharding import PartitionSpec as P

TILE = 128
MAXT = 6
H = 8
HD = 64
D = 512
OWN = 256
PAY = OWN + 16
ROWS = 16
RING = 8
BLOCKS = ROWS * 2
SLOTS = BLOCKS * 2
VROWS = 80
VBASE = D + TILE
KVROWS = VBASE + H * VROWS
ACC = D + 48
LOG2E = math.log2(math.e)
F32 = jnp.float32
BF16 = jnp.bfloat16
NEG = -1e30
GANG = 4


def split3(x):
    hi = x.astype(BF16)
    rest = x - hi.astype(F32)
    mid = rest.astype(BF16)
    low = (rest - mid.astype(F32)).astype(BF16)
    return hi, mid, low


def source_kernel(src, wk_hbm, wvt_ref, *rest):
    kv_ref, buf, wk_ref, sem, wk_sem = rest[-5:]

    def fetch(b):
        return pltpu.make_async_copy(src.at[b], buf.at[b], sem.at[b])

    weights = pltpu.make_async_copy(wk_hbm, wk_ref, wk_sem)
    weights.start()
    for b in range(2 * GANG):
        fetch(b).start()
    row = lax.broadcasted_iota(jnp.int32, (16, TILE), 0)
    ones_rows = jnp.where(row == 0, 1.0, 0.0).astype(BF16)
    r = lax.broadcasted_iota(jnp.int32, (32, 128), 0)
    c = lax.broadcasted_iota(jnp.int32, (32, 128), 1)
    select = jnp.where((c == r) & (r < 24), 1.0, 0.0).astype(BF16)

    col = lax.broadcasted_iota(jnp.int32, (TILE, TILE), 1)
    kv_ref[SLOTS] = jnp.zeros((KVROWS, TILE), BF16)
    kv_ref[SLOTS, D : D + TILE, :] = jnp.where(col < 8, NEG, 0.0).astype(BF16)
    weights.wait()

    def step(i, carry):
        for j in range(GANG):
            fetch(GANG * i + j).wait()

        @pl.when(i + 2 < BLOCKS // GANG)
        def _():
            for j in range(GANG):
                fetch(GANG * (i + 2) + j).start()

        normed = jnp.concatenate([buf[GANG * i + j, 0:OWN, :] for j in range(GANG)], axis=0)
        keys = jnp.dot(normed, wk_ref[...], preferred_element_type=F32).astype(BF16)
        vals = lax.dot_general(
            wvt_ref[...], normed, (((1,), (1,)), ((), ())), preferred_element_type=F32
        ).astype(BF16)
        prior = jnp.concatenate(
            [buf[GANG * i + j, OWN : OWN + 16, 0:OWN].astype(F32)[0:8] for j in range(GANG)], axis=1
        )
        hi, mid, low = split3(prior * LOG2E)
        stack = jnp.concatenate(
            [hi.astype(F32), mid.astype(F32), low.astype(F32), jnp.zeros((8, GANG * OWN), F32)], axis=0
        ).astype(BF16)
        aux = lax.dot_general(
            stack, select, (((0,), (0,)), ((), ())), preferred_element_type=F32
        ).astype(BF16)
        for j in range(2 * GANG):
            rows = slice(j * TILE, (j + 1) * TILE)
            t = 2 * GANG * i + j
            for p in range(4):
                kv_ref[t, p * TILE : (p + 1) * TILE, :] = keys[rows, p * 128 : (p + 1) * 128]
            kv_ref[t, D : D + TILE, :] = aux[rows, :]
            for h in range(H):
                at = VBASE + h * VROWS
                kv_ref[t, at : at + HD, :] = vals[h * HD : (h + 1) * HD, rows]
                kv_ref[t, at + HD : at + VROWS, :] = ones_rows
        return carry

    lax.fori_loop(0, BLOCKS // GANG, step, 0)


def project_source(src, w_key, w_value_t, ready):
    return pl.pallas_call(
        source_kernel,
        out_shape=pltpu.VMEM((SLOTS + 1, KVROWS, TILE), BF16),
        in_specs=[
            pl.BlockSpec(memory_space=pl.ANY),
            pl.BlockSpec(memory_space=pl.ANY),
            pl.BlockSpec(memory_space=pltpu.VMEM),
        ]
        + [pl.BlockSpec(memory_space=pl.ANY)] * len(ready),
        out_specs=pl.BlockSpec(memory_space=pltpu.VMEM),
        scratch_shapes=[
            pltpu.VMEM((BLOCKS, PAY, D), BF16),
            pltpu.VMEM((D, D), BF16),
            pltpu.SemaphoreType.DMA((BLOCKS,)),
            pltpu.SemaphoreType.DMA,
        ],
        compiler_params=pltpu.CompilerParams(vmem_limit_bytes=32 * 1024 * 1024),
        cost_estimate=pl.CostEstimate(
            flops=2 * BLOCKS * OWN * D * D * 2, bytes_accessed=BLOCKS * PAY * D * 2, transcendentals=0
        ),
        name="project_source",
    )(src, w_key, w_value_t, *ready)


def chunk_kernel(chunk, list_ref, pair_ref, q_ref, kv_ref, prev_ref, out_ref, rhs, acc, top, s_scr):
    del prev_ref
    row = lax.broadcasted_iota(jnp.int32, (TILE, 256), 0)
    col = lax.broadcasted_iota(jnp.int32, (TILE, 256), 1)
    for p in range(4):
        head = 2 * p + col // 128
        rhs[p, 0:HD, 128:256] = jnp.zeros((HD, 128), BF16)
        rhs[p, HD:128, 0:128] = jnp.zeros((HD, 128), BF16)
        rhs[p, 128:256, :] = jnp.where((row < 24) & (row % 8 == head), 1.0, 0.0).astype(BF16)

    def tile(half, carry):
        lanes = pl.ds(pl.multiple_of(half * TILE, TILE), TILE)
        for p in range(4):
            rhs[p, 0:HD, 0:128] = q_ref[p * 128 : p * 128 + HD, lanes]
            rhs[p, HD:128, 128:256] = q_ref[p * 128 + HD : (p + 1) * 128, lanes]
        base = (chunk * 2 + half) * 2 * MAXT

        def walk(count):
            tiles = [list_ref[base + j] for j in range(count)]
            peaks = [None] * 4

            def score(p):
                keys = jnp.concatenate(
                    [
                        jnp.concatenate([kv_ref[t, p * TILE : (p + 1) * TILE, :], kv_ref[t, D : D + TILE, :]], axis=1)
                        for t in tiles
                    ],
                    axis=0,
                )
                s = jnp.dot(keys, rhs[p], preferred_element_type=F32)
                s_scr[p, 0 : count * TILE, :] = s
                best = jnp.max(s.reshape(count * TILE // 8, 8, 256), axis=0)
                peaks[p] = jnp.max(best, axis=0, keepdims=True)
                top[p : p + 1, :] = peaks[p]

            def weigh(p):
                w = jnp.exp2(s_scr[p, 0 : count * TILE, :] - peaks[p]).astype(BF16)
                for g in range(2):
                    h = 2 * p + g
                    at = slice(VBASE + h * VROWS, VBASE + (h + 1) * VROWS)
                    v = jnp.concatenate([kv_ref[t, at, :] for t in tiles], axis=1)
                    o = jnp.dot(v, w[:, g * 128 : (g + 1) * 128], preferred_element_type=F32)
                    out_ref[h * HD : (h + 1) * HD, lanes] = o[0:HD, :].astype(BF16)
                    acc[h : h + 1, :] = o[HD : HD + 1, :]

            for p in range(4):
                score(p)
            for p in range(4):
                weigh(p)

        steps = (pair_ref[chunk * 2 + half] + 1) // 2
        for v in range(3):

            @pl.when(steps == v + 1)
            def _():
                walk(4 * (v + 1))

        peak = jnp.concatenate(
            [top[h // 2 : h // 2 + 1, (h % 2) * 128 : (h % 2 + 1) * 128] for h in range(H)], axis=0
        )
        t_hi, t_mid, _ = split3(acc[...])
        p_hi, p_mid, p_low = split3(peak)
        pieces = [x.astype(F32) for x in (t_hi, t_mid, p_hi, p_mid, p_low)] + [jnp.zeros((8, TILE), F32)]
        out_ref[D:ACC, lanes] = jnp.concatenate(pieces, axis=0).astype(BF16)
        return carry

    lax.fori_loop(0, 2, tile, 0)


def attend_chunk(chunk, lists, pairs, queries, source, prev):
    return pl.pallas_call(
        functools.partial(chunk_kernel, chunk),
        out_shape=jax.ShapeDtypeStruct((ACC, OWN), BF16),
        in_specs=[
            pl.BlockSpec(memory_space=pltpu.SMEM),
            pl.BlockSpec(memory_space=pltpu.SMEM),
            pl.BlockSpec(memory_space=pltpu.VMEM),
            pl.BlockSpec(memory_space=pltpu.VMEM),
            pl.BlockSpec(memory_space=pl.ANY),
        ],
        out_specs=pl.BlockSpec(memory_space=pltpu.VMEM),
        scratch_shapes=[
            pltpu.VMEM((4, 256, 256), BF16),
            pltpu.VMEM((H, TILE), F32),
            pltpu.VMEM((8, 256), F32),
            pltpu.VMEM((4, 2 * MAXT * TILE, 256), F32),
        ],
        compiler_params=pltpu.CompilerParams(vmem_limit_bytes=14 * 1024 * 1024),
        cost_estimate=pl.CostEstimate(flops=100_000_000, bytes_accessed=100_000, transcendentals=0),
        name="attend_chunk",
    )(lists, pairs, queries, source, prev)


def combine(parts):
    peaks, totals = [], []
    for ref in parts:
        aux = ref[D:ACC, :].astype(F32)
        totals.append(aux[0:8] + aux[8:16])
        peaks.append(aux[16:24] + aux[24:32] + aux[32:40])
    peak = functools.reduce(jnp.maximum, peaks)
    factors = [jnp.exp2(x - peak) for x in peaks]
    total = functools.reduce(jnp.add, [f * t for f, t in zip(factors, totals)])
    return factors, total, peak


def weighted(parts, factors, h):
    terms = [r[h * HD : (h + 1) * HD, :].astype(F32) * f[h : h + 1, :] for r, f in zip(parts, factors)]
    return functools.reduce(jnp.add, terms)


def join_kernel(a_ref, b_ref, prev_ref, out_ref):
    del prev_ref
    parts = (a_ref, b_ref)
    factors, total, peak = combine(parts)
    for h in range(H):
        out_ref[h * HD : (h + 1) * HD, :] = weighted(parts, factors, h).astype(BF16)
    t_hi, t_mid, _ = split3(total)
    p_hi, p_mid, p_low = split3(peak)
    pieces = [x.astype(F32) for x in (t_hi, t_mid, p_hi, p_mid, p_low)] + [jnp.zeros((8, OWN), F32)]
    out_ref[D:ACC, :] = jnp.concatenate(pieces, axis=0).astype(BF16)


def join(came, own, prev):
    return pl.pallas_call(
        join_kernel,
        out_shape=jax.ShapeDtypeStruct((ACC, OWN), BF16),
        in_specs=[pl.BlockSpec(memory_space=pltpu.VMEM)] * 2 + [pl.BlockSpec(memory_space=pl.ANY)],
        out_specs=pl.BlockSpec(memory_space=pltpu.VMEM),
        compiler_params=pltpu.CompilerParams(vmem_limit_bytes=14 * 1024 * 1024),
        cost_estimate=pl.CostEstimate(flops=1_000_000, bytes_accessed=100_000, transcendentals=0),
        name="join",
    )(came, own, prev)


def merge_kernel(*refs):
    parts, (ent_ref, w_ref, out_ref, att) = refs[:-4], refs[-4:]
    factors, total, _ = combine(parts)
    factors = [f / total for f in factors]
    for h in range(H):
        att[h * HD : (h + 1) * HD, :] = weighted(parts, factors, h).astype(BF16)
    out_ref[...] = ent_ref[...].astype(F32) + lax.dot_general(
        att[...], w_ref[...], (((0,), (0,)), ((), ())), preferred_element_type=F32
    )


def merge(parts, entities, w_out):
    return pl.pallas_call(
        merge_kernel,
        out_shape=jax.ShapeDtypeStruct((OWN, D), F32),
        in_specs=[pl.BlockSpec(memory_space=pltpu.VMEM)] * (len(parts) + 2),
        out_specs=pl.BlockSpec(memory_space=pltpu.VMEM),
        scratch_shapes=[pltpu.VMEM((D, OWN), BF16)],
        compiler_params=pltpu.CompilerParams(vmem_limit_bytes=14 * 1024 * 1024),
        cost_estimate=pl.CostEstimate(flops=2 * OWN * D * D, bytes_accessed=3_000_000, transcendentals=0),
        name="merge",
    )(*parts, entities, w_out)


def pack_kernel(ent_ref, bias_ref, out_ref):
    x = ent_ref[...].astype(F32)
    out_ref[0:OWN, :] = (x * lax.rsqrt(jnp.mean(x * x, axis=-1, keepdims=True) + 1e-06)).astype(BF16)
    bias = jnp.concatenate([bias_ref[...].astype(F32), jnp.zeros((8, OWN), F32)], axis=0)
    out_ref[OWN:PAY, 0:OWN] = bias.astype(BF16)
    out_ref[OWN:PAY, OWN:D] = jnp.zeros((PAY - OWN, D - OWN), BF16)


def pack(entities, entity_bias):
    return pl.pallas_call(
        pack_kernel,
        out_shape=jax.ShapeDtypeStruct((PAY, D), BF16),
        in_specs=[pl.BlockSpec(memory_space=pltpu.VMEM)] * 2,
        out_specs=pl.BlockSpec(memory_space=pltpu.VMEM),
        compiler_params=pltpu.CompilerParams(vmem_limit_bytes=14 * 1024 * 1024),
        cost_estimate=pl.CostEstimate(flops=1_000_000, bytes_accessed=600_000, transcendentals=0),
        name="pack",
    )(entities, entity_bias)


def along_z(k):
    return [(z * 2 + c, ((z + k) % RING) * 2 + c) for z in range(RING) for c in range(2)]


def across_cores():
    return [(z * 2 + c, z * 2 + 1 - c) for z in range(RING) for c in range(2)]


def neighbour_lists(tile_index, tile_count):
    me = lax.axis_index("col")
    core, z = me % 2, me // 2
    packed = jnp.concatenate([tile_index[:, 0, :], tile_count], axis=1).reshape(RING, 2, 2, MAXT + 1)
    own = lax.dynamic_index_in_dim(packed, core, 1, keepdims=False)
    other = lax.dynamic_index_in_dim(packed, 1 - core, 1, keepdims=False)
    came = lax.ppermute(other, "col", across_cores())
    first = jnp.where(core == 0, own, came)
    second = jnp.where(core == 0, came, own)

    def slots(x, group):
        t = x[..., :MAXT]
        return (t // 2 * 2 + group) * 2 + t % 2

    n0, n1 = first[..., MAXT:], second[..., MAXT:]
    pos = lax.broadcasted_iota(jnp.int32, (1, 1, 2 * MAXT), 2)
    both = jnp.concatenate([slots(first, 0), slots(second, 1)], axis=-1)
    pick = jnp.where(pos < n0, pos, MAXT + pos - n0)
    source = lax.broadcasted_iota(jnp.int32, (1, 1, 1, 2 * MAXT), 3)
    chosen = jnp.sum(jnp.where(pick[..., None] == source, both[..., None, :], 0), axis=-1)
    chosen = jnp.where(pos < n0 + n1, chosen, SLOTS)
    pairs = (n0 + n1 + 1)[..., 0] // 2
    chosen = jnp.roll(chosen, -z, axis=0)
    pairs = jnp.roll(pairs, -z, axis=0)
    return chosen.reshape(-1), pairs.reshape(-1)


def body(entities, entity_bias, w_query, w_key, w_value, w_out, tile_index, tile_count):
    payload = pack(entities, entity_bias)
    normed = payload[:OWN]
    groups = [[r * 16 + z * 2 + c for r in range(ROWS) for c in range(2)] for z in range(RING)]
    source = lax.all_gather(payload, ("row", "col"), axis=0, tiled=False, axis_index_groups=groups)

    queries = (
        lax.dot_general(w_query, normed, (((0,), (1,)), ((), ())), preferred_element_type=F32)
        * (LOG2E / math.sqrt(HD))
    ).astype(BF16)
    order = (4, 3, -3, 2, -2, 1, -1, 0)
    held = {k: lax.ppermute(queries, "col", along_z(-k)) if k else queries for k in order}
    lists, pairs = neighbour_lists(tile_index, tile_count)

    held_all = [held[k] for k in order if k]
    source = project_source(source, w_key, w_value.T, held_all)
    last = [lists]

    def chunk(k):
        last[0] = attend_chunk(k % RING, lists, pairs, held[k], source, last[0])
        return last[0]

    def joined(came, own):
        last[0] = join(came, own, last[0])
        return last[0]

    down, up = -1, 1
    send = lambda x, way: lax.ppermute(x, "col", along_z(way))
    low = send(chunk(4), down)
    high = send(chunk(3), up)
    for step in (3, 2):
        own_low = chunk(-step)
        low = send(joined(low, own_low), down)
        own_high = chunk(step - 1)
        high = send(joined(high, own_high), up)
    own_low = chunk(-1)
    low = send(joined(low, own_low), down)
    own = chunk(0)
    return merge((own, high, low), entities, w_out)


def solution(mesh):
    placed = (
        P(("row", "col"), None),
        P(None, ("row", "col")),
        P(),
        P(),
        P(),
        P(),
        P("row", "col", None),
        P("row", "col"),
    )
    return jax.shard_map(
        body, mesh=mesh, in_specs=placed, out_specs=P(("row", "col"), None), check_vma=False
    )
```

```python
import functools
import math

import jax
import jax.numpy as jnp
from jax import lax
from jax.experimental import pallas as pl
from jax.experimental.pallas import tpu as pltpu
from jax.sharding import PartitionSpec as P

TILE = 128
MAXT = 6
H = 8
HD = 64
D = 512
OWN = 256
PAY = OWN + 16
ROWS = 16
RING = 8
BLOCKS = ROWS * 2
SLOTS = BLOCKS * 2
VROWS = 80
VBASE = D + TILE
KVROWS = VBASE + H * VROWS
ACC = D + 48
LOG2E = math.log2(math.e)
F32 = jnp.float32
BF16 = jnp.bfloat16
NEG = -1e30
GANG = 4
LISTED = RING * 2 * (2 * MAXT + 1)


def split3(x):
    hi = x.astype(BF16)
    rest = x - hi.astype(F32)
    mid = rest.astype(BF16)
    low = (rest - mid.astype(F32)).astype(BF16)
    return hi, mid, low


def keep_kernel(list_in, list_ref):
    def pass_on(i, carry):
        list_ref[i] = list_in[i]
        return carry

    lax.fori_loop(0, LISTED, pass_on, 0)


def keep_lists(lists):
    return pl.pallas_call(
        keep_kernel,
        out_shape=pltpu.SMEM((LISTED,), jnp.int32),
        in_specs=[pl.BlockSpec(memory_space=pltpu.SMEM)],
        out_specs=pl.BlockSpec(memory_space=pltpu.SMEM),
        name="keep_lists",
    )(lists)


def source_kernel(src, wk_hbm, wvt_ref, *rest):
    kv_ref, buf, wk_ref, sem, wk_sem = rest[-5:]

    def fetch(b):
        return pltpu.make_async_copy(src.at[b], buf.at[b], sem.at[b])

    weights = pltpu.make_async_copy(wk_hbm, wk_ref, wk_sem)
    weights.start()
    for b in range(2 * GANG):
        fetch(b).start()
    row = lax.broadcasted_iota(jnp.int32, (16, TILE), 0)
    ones_rows = jnp.where(row == 0, 1.0, 0.0).astype(BF16)
    r = lax.broadcasted_iota(jnp.int32, (32, 128), 0)
    c = lax.broadcasted_iota(jnp.int32, (32, 128), 1)
    select = jnp.where((c == r) & (r < 24), 1.0, 0.0).astype(BF16)

    row2 = lax.broadcasted_iota(jnp.int32, (TILE, TILE), 0)
    for h in range(H):
        mine = (row2 < 24) & (row2 % 8 == h)
        kv_ref[SLOTS + 1, h * TILE : (h + 1) * TILE, :] = jnp.where(mine, 1.0, 0.0).astype(BF16)
    kv_ref[SLOTS + 1, H * TILE : KVROWS, :] = jnp.zeros((KVROWS - H * TILE, TILE), BF16)

    col = lax.broadcasted_iota(jnp.int32, (TILE, TILE), 1)
    kv_ref[SLOTS] = jnp.zeros((KVROWS, TILE), BF16)
    kv_ref[SLOTS, D : D + TILE, :] = jnp.where(col < 8, NEG, 0.0).astype(BF16)
    weights.wait()

    def step(i, carry):
        for j in range(GANG):
            fetch(GANG * i + j).wait()

        @pl.when(i + 2 < BLOCKS // GANG)
        def _():
            for j in range(GANG):
                fetch(GANG * (i + 2) + j).start()

        normed = jnp.concatenate([buf[GANG * i + j, 0:OWN, :] for j in range(GANG)], axis=0)
        keys = jnp.dot(normed, wk_ref[...], preferred_element_type=F32).astype(BF16)
        vals = lax.dot_general(
            wvt_ref[...], normed, (((1,), (1,)), ((), ())), preferred_element_type=F32
        ).astype(BF16)
        prior = jnp.concatenate(
            [buf[GANG * i + j, OWN : OWN + 16, 0:OWN].astype(F32)[0:8] for j in range(GANG)], axis=1
        )
        hi, mid, low = split3(prior * LOG2E)
        stack = jnp.concatenate(
            [hi.astype(F32), mid.astype(F32), low.astype(F32), jnp.zeros((8, GANG * OWN), F32)], axis=0
        ).astype(BF16)
        aux = lax.dot_general(
            stack, select, (((0,), (0,)), ((), ())), preferred_element_type=F32
        ).astype(BF16)
        for j in range(2 * GANG):
            rows = slice(j * TILE, (j + 1) * TILE)
            t = 2 * GANG * i + j
            for p in range(4):
                kv_ref[t, p * TILE : (p + 1) * TILE, :] = keys[rows, p * 128 : (p + 1) * 128]
            kv_ref[t, D : D + TILE, :] = aux[rows, :]
            for h in range(H):
                at = VBASE + h * VROWS
                kv_ref[t, at : at + HD, :] = vals[h * HD : (h + 1) * HD, rows]
                kv_ref[t, at + HD : at + VROWS, :] = ones_rows
        return carry

    lax.fori_loop(0, BLOCKS // GANG, step, 0)


def project_source(src, w_key, w_value_t, ready):
    return pl.pallas_call(
        source_kernel,
        out_shape=pltpu.VMEM((SLOTS + 2, KVROWS, TILE), BF16),
        in_specs=[
            pl.BlockSpec(memory_space=pl.ANY),
            pl.BlockSpec(memory_space=pl.ANY),
            pl.BlockSpec(memory_space=pltpu.VMEM),
        ]
        + [pl.BlockSpec(memory_space=pl.ANY)] * len(ready),
        out_specs=pl.BlockSpec(memory_space=pltpu.VMEM),
        scratch_shapes=[
            pltpu.VMEM((BLOCKS, PAY, D), BF16),
            pltpu.VMEM((D, D), BF16),
            pltpu.SemaphoreType.DMA((BLOCKS,)),
            pltpu.SemaphoreType.DMA,
        ],
        compiler_params=pltpu.CompilerParams(vmem_limit_bytes=32 * 1024 * 1024),
        cost_estimate=pl.CostEstimate(
            flops=2 * BLOCKS * OWN * D * D * 2, bytes_accessed=BLOCKS * PAY * D * 2, transcendentals=0
        ),
        name="project_source",
    )(src, w_key, w_value_t, *ready)


def chunk_kernel(chunk, q_ref, kv_ref, list_ref, prev_ref, out_ref, rhs, acc, top, s_scr):
    del prev_ref
    for p in range(4):
        rhs[p, 0:HD, 128:256] = jnp.zeros((HD, 128), BF16)
        rhs[p, HD:128, 0:128] = jnp.zeros((HD, 128), BF16)

    def tile(half, carry):
        lanes = pl.ds(pl.multiple_of(half * TILE, TILE), TILE)
        for p in range(4):
            rhs[p, 0:HD, 0:128] = q_ref[p * 128 : p * 128 + HD, lanes]
            rhs[p, HD:128, 128:256] = q_ref[p * 128 + HD : (p + 1) * 128, lanes]
        base = (chunk * 2 + half) * 2 * MAXT

        def walk(count):
            tiles = [list_ref[base + j] for j in range(count)]
            peaks = [None] * 4

            def score(p):
                keys = jnp.concatenate(
                    [
                        jnp.concatenate([kv_ref[t, p * TILE : (p + 1) * TILE, :], kv_ref[t, D : D + TILE, :]], axis=1)
                        for t in tiles
                    ],
                    axis=0,
                )
                extra = [kv_ref[SLOTS + 1, (2 * p + g) * TILE : (2 * p + g + 1) * TILE, :] for g in range(2)]
                right = jnp.concatenate([rhs[p], jnp.concatenate(extra, axis=1)], axis=0)
                s = jnp.dot(keys, right, preferred_element_type=F32)
                s_scr[p, 0 : count * TILE, :] = s
                best = jnp.max(s.reshape(count * TILE // 8, 8, 256), axis=0)
                peaks[p] = jnp.max(best, axis=0, keepdims=True)
                top[p : p + 1, :] = peaks[p]

            def weigh(p):
                w = jnp.exp2(s_scr[p, 0 : count * TILE, :] - peaks[p]).astype(BF16)
                for g in range(2):
                    h = 2 * p + g
                    at = slice(VBASE + h * VROWS, VBASE + (h + 1) * VROWS)
                    v = jnp.concatenate([kv_ref[t, at, :] for t in tiles], axis=1)
                    o = jnp.dot(v, w[:, g * 128 : (g + 1) * 128], preferred_element_type=F32)
                    out_ref[h * HD : (h + 1) * HD, lanes] = o[0:HD, :].astype(BF16)
                    acc[h : h + 1, :] = o[HD : HD + 1, :]

            for p in range(4):
                score(p)
            for p in range(4):
                weigh(p)

        steps = (list_ref[LISTED - 16 + chunk * 2 + half] + 1) // 2
        for v in range(3):

            @pl.when(steps == v + 1)
            def _():
                walk(4 * (v + 1))

        peak = jnp.concatenate(
            [top[h // 2 : h // 2 + 1, (h % 2) * 128 : (h % 2 + 1) * 128] for h in range(H)], axis=0
        )
        t_hi, t_mid, _ = split3(acc[...])
        p_hi, p_mid, p_low = split3(peak)
        pieces = [x.astype(F32) for x in (t_hi, t_mid, p_hi, p_mid, p_low)] + [jnp.zeros((8, TILE), F32)]
        out_ref[D:ACC, lanes] = jnp.concatenate(pieces, axis=0).astype(BF16)
        return carry

    lax.fori_loop(0, 2, tile, 0)


def attend_chunk(chunk, queries, source, lists, prev):
    return pl.pallas_call(
        functools.partial(chunk_kernel, chunk),
        out_shape=jax.ShapeDtypeStruct((ACC, OWN), BF16),
        in_specs=[pl.BlockSpec(memory_space=pltpu.VMEM)] * 2
        + [pl.BlockSpec(memory_space=pltpu.SMEM), pl.BlockSpec(memory_space=pl.ANY)],
        out_specs=pl.BlockSpec(memory_space=pltpu.VMEM),
        scratch_shapes=[
            pltpu.VMEM((4, TILE, 256), BF16),
            pltpu.VMEM((H, TILE), F32),
            pltpu.VMEM((8, 256), F32),
            pltpu.VMEM((4, 2 * MAXT * TILE, 256), F32),
        ],
        compiler_params=pltpu.CompilerParams(vmem_limit_bytes=14 * 1024 * 1024),
        cost_estimate=pl.CostEstimate(flops=100_000_000, bytes_accessed=100_000, transcendentals=0),
        name="attend_chunk",
    )(queries, source, lists, prev)


def combine(parts):
    peaks, totals = [], []
    for ref in parts:
        aux = ref[D:ACC, :].astype(F32)
        totals.append(aux[0:8] + aux[8:16])
        peaks.append(aux[16:24] + aux[24:32] + aux[32:40])
    peak = functools.reduce(jnp.maximum, peaks)
    factors = [jnp.exp2(x - peak) for x in peaks]
    total = functools.reduce(jnp.add, [f * t for f, t in zip(factors, totals)])
    return factors, total, peak


def weighted(parts, factors, h):
    terms = [r[h * HD : (h + 1) * HD, :].astype(F32) * f[h : h + 1, :] for r, f in zip(parts, factors)]
    return functools.reduce(jnp.add, terms)


def join_kernel(a_ref, b_ref, prev_ref, out_ref):
    del prev_ref
    parts = (a_ref, b_ref)
    factors, total, peak = combine(parts)
    for h in range(H):
        out_ref[h * HD : (h + 1) * HD, :] = weighted(parts, factors, h).astype(BF16)
    t_hi, t_mid, _ = split3(total)
    p_hi, p_mid, p_low = split3(peak)
    pieces = [x.astype(F32) for x in (t_hi, t_mid, p_hi, p_mid, p_low)] + [jnp.zeros((8, OWN), F32)]
    out_ref[D:ACC, :] = jnp.concatenate(pieces, axis=0).astype(BF16)


def join(came, own, prev):
    return pl.pallas_call(
        join_kernel,
        out_shape=jax.ShapeDtypeStruct((ACC, OWN), BF16),
        in_specs=[pl.BlockSpec(memory_space=pltpu.VMEM)] * 2 + [pl.BlockSpec(memory_space=pl.ANY)],
        out_specs=pl.BlockSpec(memory_space=pltpu.VMEM),
        compiler_params=pltpu.CompilerParams(vmem_limit_bytes=14 * 1024 * 1024),
        cost_estimate=pl.CostEstimate(flops=1_000_000, bytes_accessed=100_000, transcendentals=0),
        name="join",
    )(came, own, prev)


def merge_kernel(*refs):
    parts, (ent_ref, w_ref, out_ref, att) = refs[:-4], refs[-4:]
    factors, total, _ = combine(parts)
    factors = [f / total for f in factors]
    for h in range(H):
        att[h * HD : (h + 1) * HD, :] = weighted(parts, factors, h).astype(BF16)
    out_ref[...] = ent_ref[...].astype(F32) + lax.dot_general(
        att[...], w_ref[...], (((0,), (0,)), ((), ())), preferred_element_type=F32
    )


def merge(parts, entities, w_out):
    return pl.pallas_call(
        merge_kernel,
        out_shape=jax.ShapeDtypeStruct((OWN, D), F32),
        in_specs=[pl.BlockSpec(memory_space=pltpu.VMEM)] * (len(parts) + 2),
        out_specs=pl.BlockSpec(memory_space=pltpu.VMEM),
        scratch_shapes=[pltpu.VMEM((D, OWN), BF16)],
        compiler_params=pltpu.CompilerParams(vmem_limit_bytes=14 * 1024 * 1024),
        cost_estimate=pl.CostEstimate(flops=2 * OWN * D * D, bytes_accessed=3_000_000, transcendentals=0),
        name="merge",
    )(*parts, entities, w_out)


def pack_kernel(ent_ref, bias_ref, out_ref):
    x = ent_ref[...].astype(F32)
    out_ref[0:OWN, :] = (x * lax.rsqrt(jnp.mean(x * x, axis=-1, keepdims=True) + 1e-06)).astype(BF16)
    bias = jnp.concatenate([bias_ref[...].astype(F32), jnp.zeros((8, OWN), F32)], axis=0)
    out_ref[OWN:PAY, 0:OWN] = bias.astype(BF16)
    out_ref[OWN:PAY, OWN:D] = jnp.zeros((PAY - OWN, D - OWN), BF16)


def pack(entities, entity_bias):
    return pl.pallas_call(
        pack_kernel,
        out_shape=jax.ShapeDtypeStruct((PAY, D), BF16),
        in_specs=[pl.BlockSpec(memory_space=pltpu.VMEM)] * 2,
        out_specs=pl.BlockSpec(memory_space=pltpu.VMEM),
        compiler_params=pltpu.CompilerParams(vmem_limit_bytes=14 * 1024 * 1024),
        cost_estimate=pl.CostEstimate(flops=1_000_000, bytes_accessed=600_000, transcendentals=0),
        name="pack",
    )(entities, entity_bias)


def along_z(k):
    return [(z * 2 + c, ((z + k) % RING) * 2 + c) for z in range(RING) for c in range(2)]


def across_cores():
    return [(z * 2 + c, z * 2 + 1 - c) for z in range(RING) for c in range(2)]


def neighbour_lists(tile_index, tile_count):
    me = lax.axis_index("col")
    core, z = me % 2, me // 2
    packed = jnp.concatenate([tile_index[:, 0, :], tile_count], axis=1).reshape(RING, 2, 2, MAXT + 1)
    own = lax.dynamic_index_in_dim(packed, core, 1, keepdims=False)
    other = lax.dynamic_index_in_dim(packed, 1 - core, 1, keepdims=False)
    came = lax.ppermute(other, "col", across_cores())
    first = jnp.where(core == 0, own, came)
    second = jnp.where(core == 0, came, own)

    def slots(x, group):
        t = x[..., :MAXT]
        return (t // 2 * 2 + group) * 2 + t % 2

    n0, n1 = first[..., MAXT:], second[..., MAXT:]
    pos = lax.broadcasted_iota(jnp.int32, (1, 1, 2 * MAXT), 2)
    both = jnp.concatenate([slots(first, 0), slots(second, 1)], axis=-1)
    pick = jnp.where(pos < n0, pos, MAXT + pos - n0)
    source = lax.broadcasted_iota(jnp.int32, (1, 1, 1, 2 * MAXT), 3)
    chosen = jnp.sum(jnp.where(pick[..., None] == source, both[..., None, :], 0), axis=-1)
    chosen = jnp.where(pos < n0 + n1, chosen, SLOTS)
    pairs = (n0 + n1 + 1)[..., 0] // 2
    chosen = jnp.roll(chosen, -z, axis=0)
    pairs = jnp.roll(pairs, -z, axis=0)
    return jnp.concatenate([chosen.reshape(-1), pairs.reshape(-1)])


def body(entities, entity_bias, w_query, w_key, w_value, w_out, tile_index, tile_count):
    payload = pack(entities, entity_bias)
    normed = payload[:OWN]
    groups = [[r * 16 + z * 2 + c for r in range(ROWS) for c in range(2)] for z in range(RING)]
    source = lax.all_gather(payload, ("row", "col"), axis=0, tiled=False, axis_index_groups=groups)

    queries = (
        lax.dot_general(w_query, normed, (((0,), (1,)), ((), ())), preferred_element_type=F32)
        * (LOG2E / math.sqrt(HD))
    ).astype(BF16)
    order = (4, 3, -3, 2, -2, 1, -1, 0)
    held = {k: lax.ppermute(queries, "col", along_z(-k)) if k else queries for k in order}
    lists = neighbour_lists(tile_index, tile_count)

    held_all = [held[k] for k in order if k]
    source = project_source(source, w_key, w_value.T, held_all)
    kept = keep_lists(lists)
    last = [lists]

    def chunk(k):
        last[0] = attend_chunk(k % RING, held[k], source, kept, last[0])
        return last[0]

    def joined(came, own):
        last[0] = join(came, own, last[0])
        return last[0]

    down, up = -1, 1
    send = lambda x, way: lax.ppermute(x, "col", along_z(way))
    low = send(chunk(4), down)
    high = send(chunk(3), up)
    for step in (3, 2):
        own_low = chunk(-step)
        low = send(joined(low, own_low), down)
        own_high = chunk(step - 1)
        high = send(joined(high, own_high), up)
    own_low = chunk(-1)
    low = send(joined(low, own_low), down)
    own = chunk(0)
    return merge((own, high, low), entities, w_out)


def solution(mesh):
    placed = (
        P(("row", "col"), None),
        P(None, ("row", "col")),
        P(),
        P(),
        P(),
        P(),
        P("row", "col", None),
        P("row", "col"),
    )
    return jax.shard_map(
        body, mesh=mesh, in_specs=placed, out_specs=P(("row", "col"), None), check_vma=False
    )
```

```python
import functools
import math

import jax
import jax.numpy as jnp
from jax import lax
from jax.experimental import pallas as pl
from jax.experimental.pallas import tpu as pltpu
from jax.sharding import PartitionSpec as P

TILE = 128
MAXT = 6
H = 8
HD = 64
D = 512
OWN = 256
PAY = OWN + 16
ROWS = 16
RING = 8
BLOCKS = ROWS * 2
SLOTS = BLOCKS * 2
VROWS = 80
VBASE = D + TILE
KVROWS = VBASE + H * VROWS
ACC = D + 48
LOG2E = math.log2(math.e)
F32 = jnp.float32
BF16 = jnp.bfloat16
NEG = -1e30
GANG = 4
LISTED = RING * 2 * (2 * MAXT + 1)


def split3(x):
    hi = x.astype(BF16)
    rest = x - hi.astype(F32)
    mid = rest.astype(BF16)
    low = (rest - mid.astype(F32)).astype(BF16)
    return hi, mid, low


def keep_kernel(list_in, list_ref):
    def pass_on(i, carry):
        list_ref[i] = list_in[i]
        return carry

    lax.fori_loop(0, LISTED, pass_on, 0)


def keep_lists(lists):
    return pl.pallas_call(
        keep_kernel,
        out_shape=pltpu.SMEM((LISTED,), jnp.int32),
        in_specs=[pl.BlockSpec(memory_space=pltpu.SMEM)],
        out_specs=pl.BlockSpec(memory_space=pltpu.SMEM),
        name="keep_lists",
    )(lists)


def source_kernel(src, wk_hbm, wvt_ref, *rest):
    kv_ref, buf, wk_ref, sem, wk_sem = rest[-5:]

    def fetch(b):
        return pltpu.make_async_copy(src.at[b], buf.at[b], sem.at[b])

    weights = pltpu.make_async_copy(wk_hbm, wk_ref, wk_sem)
    weights.start()
    for b in range(2 * GANG):
        fetch(b).start()
    row = lax.broadcasted_iota(jnp.int32, (16, TILE), 0)
    ones_rows = jnp.where(row == 0, 1.0, 0.0).astype(BF16)
    r = lax.broadcasted_iota(jnp.int32, (32, 128), 0)
    c = lax.broadcasted_iota(jnp.int32, (32, 128), 1)
    select = jnp.where((c == r) & (r < 24), 1.0, 0.0).astype(BF16)

    row2 = lax.broadcasted_iota(jnp.int32, (TILE, TILE), 0)
    for h in range(H):
        mine = (row2 < 24) & (row2 % 8 == h)
        kv_ref[SLOTS + 1, h * TILE : (h + 1) * TILE, :] = jnp.where(mine, 1.0, 0.0).astype(BF16)
    kv_ref[SLOTS + 1, H * TILE : KVROWS, :] = jnp.zeros((KVROWS - H * TILE, TILE), BF16)

    col = lax.broadcasted_iota(jnp.int32, (TILE, TILE), 1)
    kv_ref[SLOTS] = jnp.zeros((KVROWS, TILE), BF16)
    kv_ref[SLOTS, D : D + TILE, :] = jnp.where(col < 8, NEG, 0.0).astype(BF16)
    weights.wait()

    def step(i, carry):
        for j in range(GANG):
            fetch(GANG * i + j).wait()

        @pl.when(i + 2 < BLOCKS // GANG)
        def _():
            for j in range(GANG):
                fetch(GANG * (i + 2) + j).start()

        normed = jnp.concatenate([buf[GANG * i + j, 0:OWN, :] for j in range(GANG)], axis=0)
        keys = jnp.dot(normed, wk_ref[...], preferred_element_type=F32).astype(BF16)
        vals = lax.dot_general(
            wvt_ref[...], normed, (((1,), (1,)), ((), ())), preferred_element_type=F32
        ).astype(BF16)
        prior = jnp.concatenate(
            [buf[GANG * i + j, OWN : OWN + 16, 0:OWN].astype(F32)[0:8] for j in range(GANG)], axis=1
        )
        hi, mid, low = split3(prior * LOG2E)
        stack = jnp.concatenate(
            [hi.astype(F32), mid.astype(F32), low.astype(F32), jnp.zeros((8, GANG * OWN), F32)], axis=0
        ).astype(BF16)
        aux = lax.dot_general(
            stack, select, (((0,), (0,)), ((), ())), preferred_element_type=F32
        ).astype(BF16)
        for j in range(2 * GANG):
            rows = slice(j * TILE, (j + 1) * TILE)
            t = 2 * GANG * i + j
            for p in range(4):
                kv_ref[t, p * TILE : (p + 1) * TILE, :] = keys[rows, p * 128 : (p + 1) * 128]
            kv_ref[t, D : D + TILE, :] = aux[rows, :]
            for h in range(H):
                at = VBASE + h * VROWS
                kv_ref[t, at : at + HD, :] = vals[h * HD : (h + 1) * HD, rows]
                kv_ref[t, at + HD : at + VROWS, :] = ones_rows
        return carry

    lax.fori_loop(0, BLOCKS // GANG, step, 0)


def project_source(src, w_key, w_value_t, ready):
    return pl.pallas_call(
        source_kernel,
        out_shape=pltpu.VMEM((SLOTS + 2, KVROWS, TILE), BF16),
        in_specs=[
            pl.BlockSpec(memory_space=pl.ANY),
            pl.BlockSpec(memory_space=pl.ANY),
            pl.BlockSpec(memory_space=pltpu.VMEM),
        ]
        + [pl.BlockSpec(memory_space=pl.ANY)] * len(ready),
        out_specs=pl.BlockSpec(memory_space=pltpu.VMEM),
        scratch_shapes=[
            pltpu.VMEM((BLOCKS, PAY, D), BF16),
            pltpu.VMEM((D, D), BF16),
            pltpu.SemaphoreType.DMA((BLOCKS,)),
            pltpu.SemaphoreType.DMA,
        ],
        compiler_params=pltpu.CompilerParams(vmem_limit_bytes=32 * 1024 * 1024),
        cost_estimate=pl.CostEstimate(
            flops=2 * BLOCKS * OWN * D * D * 2, bytes_accessed=BLOCKS * PAY * D * 2, transcendentals=0
        ),
        name="project_source",
    )(src, w_key, w_value_t, *ready)


def chunk_kernel(chunk, q_ref, kv_ref, list_ref, prev_ref, out_ref, rhs, acc, top, s_scr):
    del prev_ref
    for p in range(4):
        rhs[p, 0:HD, 128:256] = jnp.zeros((HD, 128), BF16)
        rhs[p, HD:128, 0:128] = jnp.zeros((HD, 128), BF16)

    def tile(half, carry):
        lanes = pl.ds(pl.multiple_of(half * TILE, TILE), TILE)
        for p in range(4):
            rhs[p, 0:HD, 0:128] = q_ref[p * 128 : p * 128 + HD, lanes]
            rhs[p, HD:128, 128:256] = q_ref[p * 128 + HD : (p + 1) * 128, lanes]
        base = (chunk * 2 + half) * 2 * MAXT

        def walk(count):
            tiles = [list_ref[base + j] for j in range(count)]
            peaks = [None] * 4

            def score(p):
                keys = jnp.concatenate(
                    [
                        jnp.concatenate([kv_ref[t, p * TILE : (p + 1) * TILE, :], kv_ref[t, D : D + TILE, :]], axis=1)
                        for t in tiles
                    ],
                    axis=0,
                )
                extra = [kv_ref[SLOTS + 1, (2 * p + g) * TILE : (2 * p + g + 1) * TILE, :] for g in range(2)]
                right = jnp.concatenate([rhs[p], jnp.concatenate(extra, axis=1)], axis=0)
                s = jnp.dot(keys, right, preferred_element_type=F32)
                s_scr[p, 0 : count * TILE, :] = s
                best = jnp.max(s.reshape(count * TILE // 8, 8, 256), axis=0)
                peaks[p] = jnp.max(best, axis=0, keepdims=True)
                top[p : p + 1, :] = peaks[p]

            def weigh(p):
                w = jnp.exp2(s_scr[p, 0 : count * TILE, :] - peaks[p]).astype(BF16)
                for g in range(2):
                    h = 2 * p + g
                    at = slice(VBASE + h * VROWS, VBASE + (h + 1) * VROWS)
                    v = jnp.concatenate([kv_ref[t, at, :] for t in tiles], axis=1)
                    o = jnp.dot(v, w[:, g * 128 : (g + 1) * 128], preferred_element_type=F32)
                    out_ref[h * HD : (h + 1) * HD, lanes] = o[0:HD, :].astype(BF16)
                    acc[h : h + 1, :] = o[HD : HD + 1, :]

            for p in range(4):
                score(p)
            for p in range(4):
                weigh(p)

        steps = (list_ref[LISTED - 16 + chunk * 2 + half] + 1) // 2
        for v in range(3):

            @pl.when(steps == v + 1)
            def _():
                walk(4 * (v + 1))

        peak = jnp.concatenate(
            [top[h // 2 : h // 2 + 1, (h % 2) * 128 : (h % 2 + 1) * 128] for h in range(H)], axis=0
        )
        t_hi, t_mid, _ = split3(acc[...])
        p_hi, p_mid, p_low = split3(peak)
        pieces = [x.astype(F32) for x in (t_hi, t_mid, p_hi, p_mid, p_low)] + [jnp.zeros((8, TILE), F32)]
        out_ref[D:ACC, lanes] = jnp.concatenate(pieces, axis=0).astype(BF16)
        return carry

    lax.fori_loop(0, 2, tile, 0)


def attend_chunk(chunk, queries, source, lists, prev):
    return pl.pallas_call(
        functools.partial(chunk_kernel, chunk),
        out_shape=jax.ShapeDtypeStruct((ACC, OWN), BF16),
        in_specs=[pl.BlockSpec(memory_space=pltpu.VMEM)] * 2
        + [pl.BlockSpec(memory_space=pltpu.SMEM), pl.BlockSpec(memory_space=pl.ANY)],
        out_specs=pl.BlockSpec(memory_space=pltpu.VMEM),
        scratch_shapes=[
            pltpu.VMEM((4, TILE, 256), BF16),
            pltpu.VMEM((H, TILE), F32),
            pltpu.VMEM((8, 256), F32),
            pltpu.VMEM((4, 2 * MAXT * TILE, 256), F32),
        ],
        compiler_params=pltpu.CompilerParams(vmem_limit_bytes=14 * 1024 * 1024),
        cost_estimate=pl.CostEstimate(flops=100_000_000, bytes_accessed=100_000, transcendentals=0),
        name="attend_chunk",
    )(queries, source, lists, prev)


def combine(parts):
    peaks, totals = [], []
    for ref in parts:
        aux = ref[D:ACC, :].astype(F32)
        totals.append(aux[0:8] + aux[8:16])
        peaks.append(aux[16:24] + aux[24:32] + aux[32:40])
    peak = functools.reduce(jnp.maximum, peaks)
    factors = [jnp.exp2(x - peak) for x in peaks]
    total = functools.reduce(jnp.add, [f * t for f, t in zip(factors, totals)])
    return factors, total, peak


def weighted(parts, factors, h):
    terms = [r[h * HD : (h + 1) * HD, :].astype(F32) * f[h : h + 1, :] for r, f in zip(parts, factors)]
    return functools.reduce(jnp.add, terms)


def join_kernel(a_ref, b_ref, prev_ref, out_ref):
    del prev_ref
    parts = (a_ref, b_ref)
    factors, total, peak = combine(parts)
    for h in range(H):
        out_ref[h * HD : (h + 1) * HD, :] = weighted(parts, factors, h).astype(BF16)
    t_hi, t_mid, _ = split3(total)
    p_hi, p_mid, p_low = split3(peak)
    pieces = [x.astype(F32) for x in (t_hi, t_mid, p_hi, p_mid, p_low)] + [jnp.zeros((8, OWN), F32)]
    out_ref[D:ACC, :] = jnp.concatenate(pieces, axis=0).astype(BF16)


def join(came, own, prev):
    return pl.pallas_call(
        join_kernel,
        out_shape=jax.ShapeDtypeStruct((ACC, OWN), BF16),
        in_specs=[pl.BlockSpec(memory_space=pltpu.VMEM)] * 2 + [pl.BlockSpec(memory_space=pl.ANY)],
        out_specs=pl.BlockSpec(memory_space=pltpu.VMEM),
        compiler_params=pltpu.CompilerParams(vmem_limit_bytes=14 * 1024 * 1024),
        cost_estimate=pl.CostEstimate(flops=1_000_000, bytes_accessed=100_000, transcendentals=0),
        name="join",
    )(came, own, prev)


def merge_kernel(*refs):
    parts, (ent_ref, w_ref, out_ref, att) = refs[:-4], refs[-4:]
    factors, total, _ = combine(parts)
    factors = [f / total for f in factors]
    for h in range(H):
        att[h * HD : (h + 1) * HD, :] = weighted(parts, factors, h).astype(BF16)
    out_ref[...] = ent_ref[...].astype(F32) + lax.dot_general(
        att[...], w_ref[...], (((0,), (0,)), ((), ())), preferred_element_type=F32
    )


def merge(parts, entities, w_out):
    return pl.pallas_call(
        merge_kernel,
        out_shape=jax.ShapeDtypeStruct((OWN, D), F32),
        in_specs=[pl.BlockSpec(memory_space=pltpu.VMEM)] * (len(parts) + 2),
        out_specs=pl.BlockSpec(memory_space=pltpu.VMEM),
        scratch_shapes=[pltpu.VMEM((D, OWN), BF16)],
        compiler_params=pltpu.CompilerParams(vmem_limit_bytes=14 * 1024 * 1024),
        cost_estimate=pl.CostEstimate(flops=2 * OWN * D * D, bytes_accessed=3_000_000, transcendentals=0),
        name="merge",
    )(*parts, entities, w_out)


def pack_kernel(ent_ref, bias_ref, out_ref):
    x = ent_ref[...].astype(F32)
    out_ref[0:OWN, :] = (x * lax.rsqrt(jnp.mean(x * x, axis=-1, keepdims=True) + 1e-06)).astype(BF16)
    bias = jnp.concatenate([bias_ref[...].astype(F32), jnp.zeros((8, OWN), F32)], axis=0)
    out_ref[OWN:PAY, 0:OWN] = bias.astype(BF16)
    out_ref[OWN:PAY, OWN:D] = jnp.zeros((PAY - OWN, D - OWN), BF16)


def pack(entities, entity_bias):
    return pl.pallas_call(
        pack_kernel,
        out_shape=jax.ShapeDtypeStruct((PAY, D), BF16),
        in_specs=[pl.BlockSpec(memory_space=pltpu.VMEM)] * 2,
        out_specs=pl.BlockSpec(memory_space=pltpu.VMEM),
        compiler_params=pltpu.CompilerParams(vmem_limit_bytes=58 * 1024 * 1024),
        cost_estimate=pl.CostEstimate(flops=1_000_000, bytes_accessed=600_000, transcendentals=0),
        name="pack",
    )(entities, entity_bias)


def along_z(k):
    return [(z * 2 + c, ((z + k) % RING) * 2 + c) for z in range(RING) for c in range(2)]


def across_cores():
    return [(z * 2 + c, z * 2 + 1 - c) for z in range(RING) for c in range(2)]


def neighbour_lists(tile_index, tile_count):
    me = lax.axis_index("col")
    core, z = me % 2, me // 2
    packed = jnp.concatenate([tile_index[:, 0, :], tile_count], axis=1).reshape(RING, 2, 2, MAXT + 1)
    own = lax.dynamic_index_in_dim(packed, core, 1, keepdims=False)
    other = lax.dynamic_index_in_dim(packed, 1 - core, 1, keepdims=False)
    came = lax.ppermute(other, "col", across_cores())
    first = jnp.where(core == 0, own, came)
    second = jnp.where(core == 0, came, own)

    def slots(x, group):
        t = x[..., :MAXT]
        return (t // 2 * 2 + group) * 2 + t % 2

    n0, n1 = first[..., MAXT:], second[..., MAXT:]
    pos = lax.broadcasted_iota(jnp.int32, (1, 1, 2 * MAXT), 2)
    both = jnp.concatenate([slots(first, 0), slots(second, 1)], axis=-1)
    pick = jnp.where(pos < n0, pos, MAXT + pos - n0)
    source = lax.broadcasted_iota(jnp.int32, (1, 1, 1, 2 * MAXT), 3)
    chosen = jnp.sum(jnp.where(pick[..., None] == source, both[..., None, :], 0), axis=-1)
    chosen = jnp.where(pos < n0 + n1, chosen, SLOTS)
    pairs = (n0 + n1 + 1)[..., 0] // 2
    chosen = jnp.roll(chosen, -z, axis=0)
    pairs = jnp.roll(pairs, -z, axis=0)
    return jnp.concatenate([chosen.reshape(-1), pairs.reshape(-1)])


def body(entities, entity_bias, w_query, w_key, w_value, w_out, tile_index, tile_count):
    payload = pack(entities, entity_bias)
    normed = payload[:OWN]
    groups = [[r * 16 + z * 2 + c for r in range(ROWS) for c in range(2)] for z in range(RING)]
    source = lax.all_gather(payload, ("row", "col"), axis=0, tiled=False, axis_index_groups=groups)

    queries = (
        lax.dot_general(w_query, normed, (((0,), (1,)), ((), ())), preferred_element_type=F32)
        * (LOG2E / math.sqrt(HD))
    ).astype(BF16)
    order = (4, 3, -3, 2, -2, 1, -1, 0)
    held = {k: lax.ppermute(queries, "col", along_z(-k)) if k else queries for k in order}
    lists = neighbour_lists(tile_index, tile_count)

    held_all = [held[k] for k in order if k]
    source = project_source(source, w_key, w_value.T, held_all)
    kept = keep_lists(lists)
    last = [lists]

    def chunk(k):
        last[0] = attend_chunk(k % RING, held[k], source, kept, last[0])
        return last[0]

    def joined(came, own):
        last[0] = join(came, own, last[0])
        return last[0]

    down, up = -1, 1
    send = lambda x, way: lax.ppermute(x, "col", along_z(way))
    low = send(chunk(4), down)
    high = send(chunk(3), up)
    for step in (3, 2):
        own_low = chunk(-step)
        low = send(joined(low, own_low), down)
        own_high = chunk(step - 1)
        high = send(joined(high, own_high), up)
    own_low = chunk(-1)
    low = send(joined(low, own_low), down)
    own = chunk(0)
    return merge((own, high, low), entities, w_out)


def solution(mesh):
    placed = (
        P(("row", "col"), None),
        P(None, ("row", "col")),
        P(),
        P(),
        P(),
        P(),
        P("row", "col", None),
        P("row", "col"),
    )
    return jax.shard_map(
        body, mesh=mesh, in_specs=placed, out_specs=P(("row", "col"), None), check_vma=False
    )
```
